32 devices in a mesh: groups: 2 (over x), attn: 8 (over z, y), ffn: 2 (over core).
Axes of the slice: x: 2, y: 2, z: 4, core: 2. Of those that a mesh axis runs over, the one named last changes fastest.
Arguments:
- queries: bfloat16 [256, 2048], P(('groups', 'attn', 'ffn')), parts along dimension 0, may hold values from -15 to 15
- kv_cache: bfloat16 [2, 262144, 128], P(None, ('groups', 'attn', 'ffn')), parts along dimension 1, may hold values from -4.2 to 4.2
- lengths: int32 [256], P(('groups', 'attn', 'ffn')), parts along dimension 0, may hold values from 1 to 2047, as said below
- hidden: bfloat16 [256, 16384], P('groups', 'attn'), parts along dimension 0, may hold values from -40 to 40
- out_weight: bfloat16 [2048, 16384], P(None, 'attn'), may hold values from -0.125 to 0.125
- norm_gain: bfloat16 [16384], P('attn'), may hold values from 0.099609375 to 1.8984375
- gate_weight: bfloat16 [16384, 3328], P('attn', 'ffn'), may hold values from -0.046875 to 0.046875
- up_weight: bfloat16 [16384, 3328], P('attn', 'ffn'), may hold values from -0.046875 to 0.046875
- down_weight: bfloat16 [3328, 16384], P('ffn', 'attn'), may hold values from -0.109375 to 0.109375
Outputs:
- updated: float32 [256, 16384], P(('groups', 'attn', 'ffn')), parts along dimension 0
The draws below stay inside these ranges and needn't reach their ends.
There are 2 independent parts, one for each index of `groups`. The reference program is written for one: setup_inputs(seed, part) draws one part's arguments, and reference() takes and returns one part's arrays. A program takes and returns all parts, laid end to end along the dimension named above; an argument that names none is the same for every part. Nothing has to cross between parts.
Inputs may be any that keep to these rules, and one draw needn't show every extreme that they name: In each aligned block of 8 requests the lengths sum to at most 8192; some block reaches 8192 and some request reaches 2047 in every draw. Slots after a block's last context hold unused entries.
All inputs are finite; a program needn't handle non-finite values.
Results may differ from the reference program's by a relative error of at most 0.0019.
Values may be sent and summed in bfloat16 or wider, within the bound.
A program may use at most 128 MiB of HBM per device.

```python
import math
import jax
import jax.numpy as jnp
from jax import lax

D = 16384
HD = 128
GQ = 16
FF = 3328
REQ_DEV = 8
TOK_DEV = 8192
REQ = 128
CACHE = 131072


def draw_queries(key, part):
    key = jax.random.fold_in(key, 11)
    first = jax.random.fold_in(key, 0)
    values = jnp.clip(jax.random.normal(first, (REQ, GQ, HD)), -4.0, 4.0)
    return values.reshape(REQ, GQ * HD).astype(jnp.bfloat16)


def draw_kv_cache(key, part):
    key = jax.random.fold_in(key, 12)
    first, second = jax.random.split(key, 2)
    keys = jnp.clip(jax.random.normal(first, (CACHE, HD)), -4.0, 4.0)
    values = jnp.clip(jax.random.normal(second, (CACHE, HD)), -4.0, 4.0)
    return jnp.stack([keys, values]).astype(jnp.bfloat16)


def draw_lengths(key, part):
    key = jax.random.fold_in(key, 13)
    first, second, third = jax.random.split(key, 3)
    blocks = REQ // REQ_DEV
    middle = TOK_DEV // REQ_DEV
    factor = jax.random.randint(first, (blocks,), 1, 9)
    full = jax.random.randint(second, (), 0, blocks)
    is_full = jnp.arange(blocks, dtype=jnp.int32) == full
    factor = jnp.where(is_full, 8, factor)
    spread = jax.random.randint(third, (blocks, REQ_DEV // 2), 0, middle)
    upper = middle + spread
    lower = middle - spread
    upper = upper.at[:, 0].set(jnp.where(is_full, 2 * middle - 1, upper[:, 0]))
    lower = lower.at[:, 0].set(jnp.where(is_full, 1, lower[:, 0]))
    base = jnp.stack([upper, lower], axis=2).reshape(blocks, REQ_DEV)
    lengths = jnp.maximum(1, base * factor[:, None] // 8)
    return lengths.reshape(REQ).astype(jnp.int32)


def draw_hidden(key, part):
    key = jax.random.fold_in(key, 14)
    first, second, third = jax.random.split(key, 3)
    row_scale = jnp.exp(jax.random.uniform(first, (REQ, 1), minval=0.0, maxval=math.log(10.0)))
    rising = jnp.exp(math.log(3.0) * jnp.arange(D, dtype=jnp.float32) / D)
    col_scale = rising[None, :] * jnp.exp(jax.random.uniform(second, (1, D), minval=0.0, maxval=math.log(10.0 / 3.0)))
    base = jnp.clip(jax.random.normal(third, (REQ, D)), -4.0, 4.0)
    return (base * row_scale * col_scale / 10.0).astype(jnp.bfloat16)


def shard_levels(own_key, dims, cuts, smallest, top_value):
    def one(position, parts):
        steps = jax.random.uniform(jax.random.fold_in(jax.random.fold_in(own_key, 6), position), (parts,), jnp.float32, smallest / len(cuts), top_value / len(cuts))
        return jnp.repeat(jnp.exp(steps), dims[position] // parts).reshape((-1,) + (1,) * (len(dims) - position - 1))

    factor_of = one(*cuts[0])
    for cut in cuts[1:]:
        factor_of = factor_of * one(*cut)
    return factor_of


def scatter_about(stream_key, extent, scale, limit, shards=(), kind=jnp.bfloat16):
    values = jax.random.normal(stream_key, extent, jnp.float32) * scale
    if len(shards) > 0:
        values = shard_levels(stream_key, extent, shards, -0.22, 0.18) * values
    return jnp.clip(values, min=-limit, max=limit).astype(kind)


def setup_inputs(seed: int = 0, part: int = 0) -> dict:
    key_of = jax.random.split(jax.random.key(seed), 10)
    part_splits = jax.random.split(jax.random.fold_in(key_of[9], part), 10)
    return {
        "queries": draw_queries(jax.random.fold_in(jax.random.fold_in(key_of[9], part), 71), part),
        "kv_cache": draw_kv_cache(jax.random.fold_in(jax.random.fold_in(key_of[9], part), 71), part),
        "lengths": draw_lengths(jax.random.fold_in(jax.random.fold_in(key_of[9], part), 71), part),
        "hidden": draw_hidden(jax.random.fold_in(jax.random.fold_in(key_of[9], part), 71), part),
        "out_weight": scatter_about(key_of[4], (GQ * HD, D), (GQ * HD) ** -0.5, 0.125, ((1, 8),)),
        "norm_gain": jnp.clip(1.0 + 0.18 * jax.random.normal(key_of[5], (D,), jnp.float32), 0.099609375, 1.8984375).astype(jnp.bfloat16),
        "gate_weight": scatter_about(key_of[6], (D, FF), D ** -0.5, 0.046875, ((0, 8), (1, 2))),
        "up_weight": scatter_about(key_of[7], (D, FF), D ** -0.5, 0.046875, ((0, 8), (1, 2))),
        "down_weight": scatter_about(key_of[8], (FF, D), FF ** -0.5, 0.109375, ((0, 2), (1, 8))),
    }


eps = 1e-05

def attend_device(pieces):
    keys, values, lens, query = pieces
    ends = jnp.cumsum(lens).astype(jnp.int32)
    starts = ends - lens
    slot = jnp.arange(TOK_DEV, dtype=jnp.int32)
    inside = (slot[None, :] >= starts[:, None]) & (slot[None, :] < ends[:, None])
    scores = jnp.einsum('rgd,td->rgt', query.astype(jnp.float32), keys.astype(jnp.float32)) / math.sqrt(HD)
    peak = lax.optimization_barrier(jnp.max(jnp.where(inside[:, None, :], scores, -jnp.inf), axis=2, keepdims=True))
    raw = jnp.where(inside[:, None, :], jnp.exp(jnp.where(inside[:, None, :], scores - peak, 0.0)), 0.0)
    total = lax.optimization_barrier(jnp.sum(raw, axis=2, keepdims=True))
    probs = raw.astype(jnp.bfloat16)
    summed = jnp.einsum('rgt,td->rgd', probs.astype(jnp.float32), values.astype(jnp.float32))
    return (summed / total).astype(jnp.bfloat16)

def reference(queries, kv_cache, lengths, hidden, out_weight, norm_gain, gate_weight, up_weight, down_weight):
    owners = REQ // REQ_DEV
    keys = kv_cache[0].reshape(owners, TOK_DEV, HD)
    values = kv_cache[1].reshape(owners, TOK_DEV, HD)
    lens = lengths.reshape(owners, REQ_DEV)
    query = queries.reshape(owners, REQ_DEV, GQ, HD)
    attended = lax.map(attend_device, (keys, values, lens, query)).reshape(REQ, GQ * HD)
    mixed = hidden.astype(jnp.float32) + jnp.dot(attended, out_weight, preferred_element_type=jnp.float32)
    inverse = lax.rsqrt(lax.optimization_barrier(jnp.mean(mixed * mixed, axis=1, keepdims=True)) + eps)
    normed = (mixed * inverse * norm_gain.astype(jnp.float32)).astype(jnp.bfloat16)
    gate = jnp.dot(normed, gate_weight, preferred_element_type=jnp.float32)
    up = jnp.dot(normed, up_weight, preferred_element_type=jnp.float32)
    units = (jax.nn.silu(gate) * up).astype(jnp.bfloat16)
    return mixed + jnp.dot(units, down_weight, preferred_element_type=jnp.float32)
```

```python
import functools
import math

import jax
import jax.numpy as jnp
from jax import lax
from jax.experimental import pallas as pl
from jax.experimental.pallas import tpu as pltpu
from jax.sharding import PartitionSpec as P

F32 = jnp.float32
BF16 = jnp.bfloat16
EPS = 1e-05
NEG = -1e30
TILES = 2


def unit_chunks(units):
    tiles = units // 128
    marks = [0, (tiles * 3) // 13, (tiles * 7) // 13, (tiles * 11) // 13, tiles]
    return [(lo * 128, (hi - lo) * 128) for lo, hi in zip(marks, marks[1:])]


def fold(x):
    half = x.shape[1] // 2
    return jnp.concatenate([x[:, :half], x[:, half:]], axis=0)


def unfold(x):
    rows = x.shape[0] // 2
    return jnp.concatenate([x[:rows], x[rows:]], axis=1)


def kernel(n, names, *refs):
    (q_ref, kv_ref, len_ref, hid_ref, wo_ref, gain_ref, wg_ref, wu_ref, wd_ref, out_ref) = refs[:10]
    s = dict(zip(names, refs[10:]))
    a = lax.axis_index("attn")
    f = lax.axis_index("ffn")
    nh = n // 2
    me = a * 2 + f
    pa = lax.rem(a, 2)
    ja = a // 2
    partner = {"attn": a + 1 - 2 * pa, "ffn": f}
    sibling = {"attn": a, "ffn": 1 - f}
    req, width = q_ref.shape
    slots, hd = s["k"].shape
    heads = width // hd
    rows = n * 16
    cols = hid_ref.shape[1]
    units = wg_ref.shape[1]
    cuts = unit_chunks(units)
    tw = cols // TILES

    def remote(src, dst, ssem, rsem, dev):
        return pltpu.make_async_remote_copy(
            src_ref=src, dst_ref=dst, send_sem=ssem, recv_sem=rsem,
            device_id=dev, device_id_type=pl.DeviceIdType.MESH)

    def local(src, dst, i):
        return pltpu.make_async_copy(src, dst, s["loc"].at[i])

    cp_k = local(kv_ref.at[0], s["k"], 0)
    cp_v = local(kv_ref.at[1], s["v"], 1)
    cp_h = local(hid_ref, s["hid"], 2)
    cp_o = local(wo_ref, s["wo"], 3)
    cp_g = local(wg_ref, s["wg"], 4)
    cp_u = local(wu_ref, s["wu"], 5)
    cp_d = local(wd_ref, s["wd"], 6)
    cp_h.start()
    cp_k.start()
    cp_v.start()

    barrier = pltpu.get_barrier_semaphore()

    @pl.loop(1, 2 * n)
    def _(i):
        d = lax.rem(me + i, 2 * n)
        pl.semaphore_signal(barrier, inc=1, device_id={"attn": d // 2, "ffn": lax.rem(d, 2)},
                            device_id_type=pl.DeviceIdType.MESH)

    cp_h.wait()
    pl.semaphore_wait(barrier, 2 * n - 1)

    def own_rows(b):
        blk = s["hid"][pl.ds(pl.multiple_of(b * 16, 16), 16), :].astype(F32)
        return jnp.where(f == 0, blk[:8], blk[8:])

    def hid_copy(b):
        return remote(s["hid_send"].at[b], s["hid_recv"].at[a], s["hid_s"].at[b], s["hid_r"].at[a],
                      {"attn": b, "ffn": f})

    x = own_rows(a)
    for t in range(TILES):
        s["hid_recv"][a, t] = fold(x[:, t * tw:(t + 1) * tw]).astype(BF16)

    @pl.loop(1, n)
    def _(i):
        b = lax.rem(a + i, n)
        x = own_rows(b)
        for t in range(TILES):
            s["hid_send"][b, t] = fold(x[:, t * tw:(t + 1) * tw]).astype(BF16)
        hid_copy(b).start()

    q32 = q_ref[...].astype(F32)
    qs = jnp.concatenate([q32[:, g * hd:(g + 1) * hd] for g in range(heads)], axis=0).astype(BF16)
    at_row = lax.broadcasted_iota(jnp.int32, (req, 1), 0)
    starts = jnp.zeros((req, 1), jnp.int32)
    ends = jnp.zeros((req, 1), jnp.int32)
    run = jnp.int32(0)
    for i in range(req):
        starts = jnp.where(at_row == i, run, starts)
        run = run + len_ref[i]
        ends = jnp.where(at_row == i, run, ends)
    tc = min(1024, slots)
    qr = req * heads
    cp_k.wait()
    cp_o.start()

    def first(k, m):
        off = pl.multiple_of(k * tc, tc)
        sc = lax.dot_general(qs, s["k"][pl.ds(off, tc), :], (((1,), (1,)), ((), ())),
                             preferred_element_type=F32)
        slot = off + lax.broadcasted_iota(jnp.int32, (req, tc), 1)
        inside = (slot >= starts) & (slot < ends)
        sc = jnp.where(inside[None], sc.reshape(heads, req, tc), NEG).reshape(qr, tc)
        s["sc"][:, pl.ds(off, tc)] = sc
        for t in range(tc // 128):
            m = jnp.maximum(m, sc[:, t * 128:(t + 1) * 128])
        return m

    m = lax.fori_loop(0, slots // tc, first, jnp.full((qr, 128), NEG, F32))
    peak = jnp.max(m, axis=1, keepdims=True)
    cp_v.wait()
    cp_g.start()
    cp_u.start()
    cp_d.start()

    scale2 = 1.4426950408889634 / math.sqrt(hd)

    def second(k, carry):
        tot, acc = carry
        off = pl.multiple_of(k * tc, tc)
        p = jnp.exp2((s["sc"][:, pl.ds(off, tc)] - peak) * scale2)
        for t in range(tc // 128):
            tot = tot + p[:, t * 128:(t + 1) * 128]
        acc = acc + jnp.dot(p.astype(BF16), s["v"][pl.ds(off, tc), :], preferred_element_type=F32)
        return tot, acc

    tot, acc = lax.fori_loop(0, slots // tc, second,
                             (jnp.zeros((qr, 128), F32), jnp.zeros((qr, hd), F32)))
    att = acc / jnp.sum(tot, axis=1, keepdims=True)
    att = jnp.concatenate([att[g * req:(g + 1) * req] for g in range(heads)], axis=1)
    s["att"][ja, pa, f] = fold(att).astype(BF16)

    def aa_copy(j):
        blk = s["att"].at[ja, pa, f]
        return remote(blk, blk, s["aa_s"].at[j], s["aa_r"].at[ja], {"attn": 2 * j + pa, "ffn": f})

    def ab_copy(j):
        blk = s["att"].at[j, pa, f]
        return remote(blk, blk, s["ab_s"].at[j], s["ab_r"].at[j], partner)

    def ac_copy(j, par):
        blk = s["att"].at[j, par, f]
        return remote(blk, blk, s["ac_s"].at[j, par], s["ac_r"].at[j, par], sibling)

    @pl.loop(1, nh)
    def _(i):
        aa_copy(lax.rem(ja + i, nh)).start()

    ab_copy(ja).start()
    ac_copy(ja, pa).start()

    @pl.loop(1, nh)
    def _(i):
        j = lax.rem(ja + i, nh)
        blk = s["att"].at[j, pa, f]
        remote(blk, blk, s["aa_s"].at[j], s["aa_r"].at[j], {"attn": 2 * j + pa, "ffn": f}).wait_recv()
        ab_copy(j).start()
        ac_copy(j, pa).start()

    @pl.loop(0, nh)
    def _(i):
        j = lax.rem(ja + i, nh)
        blk = s["att"].at[j, 1 - pa, f]
        remote(blk, blk, s["ab_s"].at[j], s["ab_r"].at[j], partner).wait_recv()
        ac_copy(j, 1 - pa).start()

    @pl.loop(0, nh)
    def _(i):
        j = lax.rem(ja + i, nh)
        for k in range(2):
            par = pa if k == 0 else 1 - pa
            blk = s["att"].at[j, par, 1 - f]
            remote(blk, blk, s["ac_s"].at[j, par], s["ac_r"].at[j, par], sibling).wait_recv()

    @pl.loop(0, n)
    def _(p):
        pair = [unfold(s["att"][p // 2, lax.rem(p, 2), k].astype(F32)) for k in range(2)]
        s["heads_in"][pl.ds(pl.multiple_of(p * 16, 16), 16), :] = jnp.concatenate(pair, axis=0).astype(BF16)

    cp_o.wait()
    mt = min(512, cols)

    def project(t, sq):
        c = pl.ds(pl.multiple_of(t * mt, mt), mt)
        hp = jnp.dot(s["heads_in"][...], s["wo"][:, c], preferred_element_type=F32)
        s["heads"][:, c] = hp
        mx = hp + s["hid"][:, c].astype(F32)
        s["h"][:, c] = (mx * gain_ref[c].astype(F32).reshape(1, mt)).astype(BF16)
        for k in range(mt // 128):
            y = mx[:, k * 128:(k + 1) * 128]
            sq = sq + y * y
        return sq

    sq = lax.fori_loop(0, cols // mt, project, jnp.zeros((rows, 128), F32))
    sq = jnp.broadcast_to(jnp.sum(sq, axis=1, keepdims=True), (rows, 128))
    s["sq_recv"][a] = jnp.transpose(sq)[:8]

    def sq_copy(b):
        return remote(s["sq_recv"].at[a], s["sq_recv"].at[a], s["sq_s"].at[b], s["sq_r"].at[a],
                      {"attn": b, "ffn": f})

    @pl.loop(1, n)
    def _(i):
        sq_copy(lax.rem(a + i, n)).start()

    def s1_copy(c):
        return remote(s["s1_send%d" % c], s["s1_recv%d" % c], s["s1_s"].at[c], s["s1_r"].at[c], partner)

    def s2_copy(c, j):
        return remote(s["s2_send%d" % c].at[j], s["s2_recv%d" % c].at[ja], s["s2_s"].at[c, j], s["s2_r"].at[c, ja],
                      {"attn": 2 * j + pa, "ffn": f})

    def ua_copy(c, j):
        blk = s["u%d" % c].at[ja, pa]
        return remote(blk, blk, s["ua_s"].at[c, j], s["ua_r"].at[c, ja], {"attn": 2 * j + pa, "ffn": f})

    def ub_copy(c, j):
        blk = s["u%d" % c].at[j, pa]
        return remote(blk, blk, s["ub_s"].at[c, j], s["ub_r"].at[c, j], partner)

    def gate_up(c):
        at, w = cuts[c]
        part = s["part%d" % c]
        for k, wt in enumerate(("wg", "wu")):
            r = jnp.dot(s["h"][...], s[wt][:, at:at + w], preferred_element_type=F32)
            part[:, :, :, k * w:(k + 1) * w] = r.reshape(nh, 2, 16, w)

        @pl.loop(0, nh)
        def _(j):
            s["s1_send%d" % c][j] = part[j, 1 - pa].astype(BF16)

        s1_copy(c).start()

    def pair_sum(c):
        s1_copy(c).wait_recv()
        part = s["part%d" % c]

        @pl.loop(1, nh)
        def _(i):
            j = lax.rem(ja + i, nh)
            s["s2_send%d" % c][j] = (part[j, pa] + s["s1_recv%d" % c][j].astype(F32)).astype(BF16)
            s2_copy(c, j).start()

    def make_units(c, inv):
        at, w = cuts[c]
        total = s["part%d" % c][ja, pa] + s["s1_recv%d" % c][ja].astype(F32)

        def body(i, total):
            j = lax.rem(ja + i, nh)
            blk = s["s2_recv%d" % c].at[j]
            remote(blk, blk, s["s2_s"].at[c, j], s["s2_r"].at[c, j], {"attn": 2 * j + pa, "ffn": f}).wait_recv()
            return total + blk[...].astype(F32)

        total = lax.fori_loop(1, nh, body, total)
        gate = total[:, :w] * inv
        up = total[:, w:] * inv
        s["u%d" % c][ja, pa] = (gate / (1.0 + jnp.exp(-gate)) * up).astype(BF16)

        @pl.loop(1, nh)
        def _(i):
            ua_copy(c, lax.rem(ja + i, nh)).start()

        ub_copy(c, ja).start()

    def forward(c):
        @pl.loop(1, nh)
        def _(i):
            j = lax.rem(ja + i, nh)
            blk = s["u%d" % c].at[j, pa]
            remote(blk, blk, s["ua_s"].at[c, j], s["ua_r"].at[c, j], {"attn": 2 * j + pa, "ffn": f}).wait_recv()
            ub_copy(c, j).start()

    def take_units(c):
        @pl.loop(0, nh)
        def _(j):
            blk = s["u%d" % c].at[j, 1 - pa]
            remote(blk, blk, s["ub_s"].at[c, j], s["ub_r"].at[c, j], partner).wait_recv()

    def down(c, t):
        at, w = cuts[c]
        mtd = min(512, tw)
        u = s["u%d" % c][...].reshape(rows, w)

        @pl.loop(0, tw // mtd)
        def _(k):
            col = pl.ds(pl.multiple_of(t * tw + k * mtd, mtd), mtd)
            loc = pl.ds(pl.multiple_of(k * mtd, mtd), mtd)
            r = jnp.dot(u, s["wd"][at:at + w, col], preferred_element_type=F32).reshape(n, 2, 8, mtd)
            if c > 0:
                r = r + s["down"][t, :, :, :, loc]
            s["down"][t, :, :, :, loc] = r

    cp_g.wait()
    cp_u.wait()
    gate_up(0)

    @pl.loop(1, n)
    def _(i):
        b = lax.rem(a + i, n)
        blk = s["sq_recv"].at[b]
        remote(blk, blk, s["sq_s"].at[b], s["sq_r"].at[b], {"attn": b, "ffn": f}).wait_recv()

    inv = lax.rsqrt(jnp.sum(s["sq_recv"][...], axis=0)[:1] / (n * cols) + EPS)
    s["inv"][...] = jnp.transpose(jnp.broadcast_to(inv, (128, rows)))

    @pl.loop(0, cols // mt)
    def _(t):
        c = pl.ds(pl.multiple_of(t * mt, mt), mt)
        mx = s["heads"][:, c] + s["hid"][:, c].astype(F32)
        s["h"][:, c] = (mx * s["inv"][:, :1] * gain_ref[c].astype(F32).reshape(1, mt)).astype(BF16)

    own_inv = s["inv"][pl.ds(pl.multiple_of(a * 16, 16), 16), :1]
    gate_up(1)
    pair_sum(0)
    gate_up(2)
    pair_sum(1)
    gate_up(3)
    make_units(0, own_inv)
    pair_sum(2)
    make_units(1, 1.0)
    forward(0)
    pair_sum(3)
    make_units(2, 1.0)
    forward(1)
    cp_d.wait()
    take_units(0)
    for t in range(TILES):
        down(0, t)
    make_units(3, 1.0)
    forward(2)
    take_units(1)
    for t in range(TILES):
        down(1, t)
    forward(3)
    take_units(2)
    for t in range(TILES):
        down(2, t)
    take_units(3)

    def sib_copy(t):
        return remote(s["down"].at[t, :, 1 - f], s["sib_recv"].at[t], s["sib_s"].at[t], s["sib_r"].at[t], sibling)

    def fin_copy(t, b):
        return remote(s["fin_send"].at[t, b], s["fin_recv"].at[t, a], s["fin_s"].at[t, b], s["fin_r"].at[t, a],
                      {"attn": b, "ffn": f})

    for t in range(TILES):
        down(3, t)
        sib_copy(t).start()
    for t in range(TILES):
        sib_copy(t).wait_recv()

        def added(b):
            hp = s["heads"][pl.ds(pl.multiple_of(b * 16, 16), 16), t * tw:(t + 1) * tw]
            hp = jnp.where(f == 0, hp[:8], hp[8:])
            return fold(s["down"][t, b, f] + s["sib_recv"][t, b] + hp)

        @pl.loop(1, n)
        def _(i):
            b = lax.rem(a + i, n)
            s["fin_send"][t, b] = added(b).astype(BF16)
            fin_copy(t, b).start()

        s["fin_recv"][t, a] = added(a).astype(BF16)

    def put(b):
        for t in range(TILES):
            y = unfold(s["hid_recv"][b, t].astype(F32) + s["fin_recv"][t, b].astype(F32))
            out_ref[:, pl.ds(pl.multiple_of(b * cols + t * tw, tw), tw)] = y

    put(a)

    @pl.loop(1, n)
    def _(i):
        b = lax.rem(a + i, n)
        blk = s["hid_recv"].at[b]
        remote(blk, blk, s["hid_s"].at[b], s["hid_r"].at[b], {"attn": b, "ffn": f}).wait_recv()
        for t in range(TILES):
            blk = s["fin_recv"].at[t, b]
            remote(blk, blk, s["fin_s"].at[t, b], s["fin_r"].at[t, b], {"attn": b, "ffn": f}).wait_recv()
        put(b)

    @pl.loop(1, nh)
    def _(i):
        aa_copy(lax.rem(ja + i, nh)).wait_send()

    @pl.loop(0, nh)
    def _(j):
        ab_copy(j).wait_send()
        for par in range(2):
            ac_copy(j, par).wait_send()

    @pl.loop(1, n)
    def _(i):
        b = lax.rem(a + i, n)
        hid_copy(b).wait_send()
        sq_copy(b).wait_send()
        for t in range(TILES):
            fin_copy(t, b).wait_send()

    for c in range(len(cuts)):
        s1_copy(c).wait_send()
        ub_copy(c, ja).wait_send()

        @pl.loop(1, nh)
        def _(i):
            j = lax.rem(ja + i, nh)
            s2_copy(c, j).wait_send()
            ua_copy(c, j).wait_send()
            ub_copy(c, j).wait_send()

    for t in range(TILES):
        sib_copy(t).wait_send()


def per_device(n, queries, kv_cache, lengths, hidden, out_weight, norm_gain, gate_weight, up_weight, down_weight):
    req, width = queries.shape
    slots, hd = kv_cache.shape[1:]
    rows, cols = hidden.shape
    units = gate_weight.shape[1]
    nh = n // 2
    tw = cols // TILES
    cuts = unit_chunks(units)
    nc = len(cuts)
    V, D = pltpu.VMEM, pltpu.SemaphoreType.DMA
    sc = {
        "k": V((slots, hd), BF16), "v": V((slots, hd), BF16), "hid": V((rows, cols), BF16),
        "wo": V(out_weight.shape, BF16), "wg": V(gate_weight.shape, BF16), "wu": V(up_weight.shape, BF16),
        "wd": V(down_weight.shape, BF16), "sc": V((req * width // hd, slots), F32),
        "hid_send": V((n, TILES, 16, tw // 2), BF16), "hid_recv": V((n, TILES, 16, tw // 2), BF16),
        "att": V((nh, 2, 2, 16, width // 2), BF16), "heads_in": V((rows, width), BF16),
        "heads": V((rows, cols), F32), "h": V((rows, cols), BF16),
        "sq_recv": V((n, 8, rows), F32), "inv": V((rows, 128), F32),
        "down": V((TILES, n, 2, 8, tw), F32), "sib_recv": V((TILES, n, 8, tw), F32),
        "fin_send": V((TILES, n, 16, tw // 2), BF16), "fin_recv": V((TILES, n, 16, tw // 2), BF16),
        "loc": D((7,)), "aa_s": D((nh,)), "aa_r": D((nh,)), "ab_s": D((nh,)), "ab_r": D((nh,)),
        "ac_s": D((nh, 2)), "ac_r": D((nh, 2)), "hid_s": D((n,)), "hid_r": D((n,)),
        "sq_s": D((n,)), "sq_r": D((n,)), "s1_s": D((nc,)), "s1_r": D((nc,)),
        "s2_s": D((nc, nh)), "s2_r": D((nc, nh)), "ua_s": D((nc, nh)), "ua_r": D((nc, nh)),
        "ub_s": D((nc, nh)), "ub_r": D((nc, nh)), "sib_s": D((TILES,)), "sib_r": D((TILES,)),
        "fin_s": D((TILES, n)), "fin_r": D((TILES, n)),
    }
    for c, (_, w) in enumerate(cuts):
        sc["part%d" % c] = V((nh, 2, 16, 2 * w), F32)
        for name in ("s1_send", "s1_recv", "s2_send", "s2_recv"):
            sc["%s%d" % (name, c)] = V((nh, 16, 2 * w), BF16)
        sc["u%d" % c] = V((nh, 2, 16, w), BF16)
    hbm = pl.BlockSpec(memory_space=pl.ANY)
    vmem = pl.BlockSpec(memory_space=pltpu.VMEM)
    smem = pl.BlockSpec(memory_space=pltpu.SMEM)
    return pl.pallas_call(
        functools.partial(kernel, n, tuple(sc)),
        out_shape=jax.ShapeDtypeStruct((req, cols * n), F32),
        in_specs=[vmem, hbm, smem, hbm, hbm, vmem, hbm, hbm, hbm],
        out_specs=vmem,
        scratch_shapes=list(sc.values()),
        compiler_params=pltpu.CompilerParams(collective_id=0, has_side_effects=True,
                                             vmem_limit_bytes=58 * 1024 * 1024),
    )(queries, kv_cache, lengths, hidden, out_weight, norm_gain, gate_weight, up_weight, down_weight)


def solution(mesh):
    return jax.shard_map(
        functools.partial(per_device, mesh.shape["attn"]),
        mesh=mesh,
        in_specs=(
            P(("groups", "attn", "ffn"), None),
            P(None, ("groups", "attn", "ffn"), None),
            P(("groups", "attn", "ffn")),
            P("groups", "attn"),
            P(None, "attn"),
            P("attn"),
            P("attn", "ffn"),
            P("attn", "ffn"),
            P("ffn", "attn"),
        ),
        out_specs=P(("groups", "attn", "ffn"), None),
        check_vma=False,
    )
```

```python
import functools
import math

import jax
import jax.numpy as jnp
from jax import lax
from jax.experimental import pallas as pl
from jax.experimental.pallas import tpu as pltpu
from jax.sharding import PartitionSpec as P

F32 = jnp.float32
BF16 = jnp.bfloat16
EPS = 1e-05
NEG = -1e30
TILES = 2


def unit_chunks(units):
    tiles = units // 128
    marks = [0, (tiles * 2) // 13, (tiles * 6) // 13, (tiles * 10) // 13, tiles]
    return [(lo * 128, (hi - lo) * 128) for lo, hi in zip(marks, marks[1:])]


def fold(x):
    half = x.shape[1] // 2
    return jnp.concatenate([x[:, :half], x[:, half:]], axis=0)


def unfold(x):
    rows = x.shape[0] // 2
    return jnp.concatenate([x[:rows], x[rows:]], axis=1)


def kernel(n, names, *refs):
    (q_ref, kv_ref, len_ref, hid_ref, wo_ref, gain_ref, wg_ref, wu_ref, wd_ref, out_ref) = refs[:10]
    s = dict(zip(names, refs[10:]))
    a = lax.axis_index("attn")
    f = lax.axis_index("ffn")
    nh = n // 2
    me = a * 2 + f
    pa = lax.rem(a, 2)
    ja = a // 2
    partner = {"attn": a + 1 - 2 * pa, "ffn": f}
    sibling = {"attn": a, "ffn": 1 - f}
    req, width = q_ref.shape
    slots, hd = s["k"].shape
    heads = width // hd
    rows = n * 16
    cols = hid_ref.shape[1]
    units = wg_ref.shape[1]
    cuts = unit_chunks(units)
    tw = cols // TILES

    def remote(src, dst, ssem, rsem, dev):
        return pltpu.make_async_remote_copy(
            src_ref=src, dst_ref=dst, send_sem=ssem, recv_sem=rsem,
            device_id=dev, device_id_type=pl.DeviceIdType.MESH)

    def local(src, dst, i):
        return pltpu.make_async_copy(src, dst, s["loc"].at[i])

    cp_k = local(kv_ref.at[0], s["k"], 0)
    cp_v = local(kv_ref.at[1], s["v"], 1)
    cp_h = local(hid_ref, s["hid"], 2)
    cp_o = local(wo_ref, s["wo"], 3)
    cp_g = local(wg_ref, s["wg"], 4)
    cp_u = local(wu_ref, s["wu"], 5)
    cp_d = local(wd_ref, s["wd"], 6)
    cp_h.start()
    cp_k.start()
    cp_v.start()

    barrier = pltpu.get_barrier_semaphore()

    @pl.loop(1, 2 * n)
    def _(i):
        d = lax.rem(me + i, 2 * n)
        pl.semaphore_signal(barrier, inc=1, device_id={"attn": d // 2, "ffn": lax.rem(d, 2)},
                            device_id_type=pl.DeviceIdType.MESH)

    cp_h.wait()
    pl.semaphore_wait(barrier, 2 * n - 1)

    def own_rows(b):
        blk = s["hid"][pl.ds(pl.multiple_of(b * 16, 16), 16), :].astype(F32)
        return jnp.where(f == 0, blk[:8], blk[8:])

    def hid_copy(b):
        return remote(s["hid_send"].at[b], s["hid_recv"].at[a], s["hid_s"].at[b], s["hid_r"].at[a],
                      {"attn": b, "ffn": f})

    x = own_rows(a)
    for t in range(TILES):
        s["hid_recv"][a, t] = fold(x[:, t * tw:(t + 1) * tw]).astype(BF16)

    @pl.loop(1, n)
    def _(i):
        b = lax.rem(a + i, n)
        x = own_rows(b)
        for t in range(TILES):
            s["hid_send"][b, t] = fold(x[:, t * tw:(t + 1) * tw]).astype(BF16)
        hid_copy(b).start()

    q32 = q_ref[...].astype(F32)
    qs = jnp.concatenate([q32[:, g * hd:(g + 1) * hd] for g in range(heads)], axis=0).astype(BF16)
    at_row = lax.broadcasted_iota(jnp.int32, (req, 1), 0)
    starts = jnp.zeros((req, 1), jnp.int32)
    ends = jnp.zeros((req, 1), jnp.int32)
    run = jnp.int32(0)
    for i in range(req):
        starts = jnp.where(at_row == i, run, starts)
        run = run + len_ref[i]
        ends = jnp.where(at_row == i, run, ends)
    tc = min(1024, slots)
    qr = req * heads
    cp_k.wait()
    cp_o.start()
    cp_g.start()
    cp_u.start()
    cp_d.start()

    def first(k, m):
        off = pl.multiple_of(k * tc, tc)
        sc = lax.dot_general(qs, s["k"][pl.ds(off, tc), :], (((1,), (1,)), ((), ())),
                             preferred_element_type=F32)
        slot = off + lax.broadcasted_iota(jnp.int32, (req, tc), 1)
        inside = (slot >= starts) & (slot < ends)
        sc = jnp.where(inside[None], sc.reshape(heads, req, tc), NEG).reshape(qr, tc)
        s["sc"][:, pl.ds(off, tc)] = sc
        for t in range(tc // 128):
            m = jnp.maximum(m, sc[:, t * 128:(t + 1) * 128])
        return m

    m = lax.fori_loop(0, slots // tc, first, jnp.full((qr, 128), NEG, F32))
    peak = jnp.max(m, axis=1, keepdims=True)
    cp_v.wait()

    scale2 = 1.4426950408889634 / math.sqrt(hd)

    def second(k, carry):
        tot, acc = carry
        off = pl.multiple_of(k * tc, tc)
        p = jnp.exp2((s["sc"][:, pl.ds(off, tc)] - peak) * scale2)
        for t in range(tc // 128):
            tot = tot + p[:, t * 128:(t + 1) * 128]
        acc = acc + jnp.dot(p.astype(BF16), s["v"][pl.ds(off, tc), :], preferred_element_type=F32)
        return tot, acc

    tot, acc = lax.fori_loop(0, slots // tc, second,
                             (jnp.zeros((qr, 128), F32), jnp.zeros((qr, hd), F32)))
    att = acc / jnp.sum(tot, axis=1, keepdims=True)
    att = jnp.concatenate([att[g * req:(g + 1) * req] for g in range(heads)], axis=1)
    s["att"][ja, pa, f] = fold(att).astype(BF16)

    def aa_copy(j):
        blk = s["att"].at[ja, pa, f]
        return remote(blk, blk, s["aa_s"].at[j], s["aa_r"].at[ja], {"attn": 2 * j + pa, "ffn": f})

    def ab_copy(j):
        blk = s["att"].at[j, pa, f]
        return remote(blk, blk, s["ab_s"].at[j], s["ab_r"].at[j], partner)

    def ac_copy(j, par):
        blk = s["att"].at[j, par, f]
        return remote(blk, blk, s["ac_s"].at[j, par], s["ac_r"].at[j, par], sibling)

    @pl.loop(1, nh)
    def _(i):
        aa_copy(lax.rem(ja + i, nh)).start()

    ab_copy(ja).start()
    ac_copy(ja, pa).start()

    @pl.loop(1, nh)
    def _(i):
        j = lax.rem(ja + i, nh)
        blk = s["att"].at[j, pa, f]
        remote(blk, blk, s["aa_s"].at[j], s["aa_r"].at[j], {"attn": 2 * j + pa, "ffn": f}).wait_recv()
        ab_copy(j).start()
        ac_copy(j, pa).start()

    @pl.loop(0, nh)
    def _(i):
        j = lax.rem(ja + i, nh)
        blk = s["att"].at[j, 1 - pa, f]
        remote(blk, blk, s["ab_s"].at[j], s["ab_r"].at[j], partner).wait_recv()
        ac_copy(j, 1 - pa).start()

    @pl.loop(0, nh)
    def _(i):
        j = lax.rem(ja + i, nh)
        for k in range(2):
            par = pa if k == 0 else 1 - pa
            blk = s["att"].at[j, par, 1 - f]
            remote(blk, blk, s["ac_s"].at[j, par], s["ac_r"].at[j, par], sibling).wait_recv()

    @pl.loop(0, n)
    def _(p):
        pair = [unfold(s["att"][p // 2, lax.rem(p, 2), k].astype(F32)) for k in range(2)]
        s["heads_in"][pl.ds(pl.multiple_of(p * 16, 16), 16), :] = jnp.concatenate(pair, axis=0).astype(BF16)

    cp_o.wait()
    mt = min(512, cols)

    def project(t, sq):
        c = pl.ds(pl.multiple_of(t * mt, mt), mt)
        hp = jnp.dot(s["heads_in"][...], s["wo"][:, c], preferred_element_type=F32)
        s["heads"][:, c] = hp
        mx = hp + s["hid"][:, c].astype(F32)
        s["h"][:, c] = (mx * gain_ref[c].astype(F32).reshape(1, mt)).astype(BF16)
        for k in range(mt // 128):
            y = mx[:, k * 128:(k + 1) * 128]
            sq = sq + y * y
        return sq

    sq = lax.fori_loop(0, cols // mt, project, jnp.zeros((rows, 128), F32))
    sq = jnp.broadcast_to(jnp.sum(sq, axis=1, keepdims=True), (rows, 128))
    s["sq_recv"][a] = jnp.transpose(sq)[:8]

    def sq_copy(b):
        return remote(s["sq_recv"].at[a], s["sq_recv"].at[a], s["sq_s"].at[b], s["sq_r"].at[a],
                      {"attn": b, "ffn": f})

    @pl.loop(1, n)
    def _(i):
        sq_copy(lax.rem(a + i, n)).start()

    def s1_copy(c):
        return remote(s["s1_send%d" % c], s["s1_recv%d" % c], s["s1_s"].at[c], s["s1_r"].at[c], partner)

    def s2_copy(c, j):
        return remote(s["s2_send%d" % c].at[j], s["s2_recv%d" % c].at[ja], s["s2_s"].at[c, j], s["s2_r"].at[c, ja],
                      {"attn": 2 * j + pa, "ffn": f})

    def ua_copy(c, j):
        blk = s["u%d" % c].at[ja, pa]
        return remote(blk, blk, s["ua_s"].at[c, j], s["ua_r"].at[c, ja], {"attn": 2 * j + pa, "ffn": f})

    def ub_copy(c, j):
        blk = s["u%d" % c].at[j, pa]
        return remote(blk, blk, s["ub_s"].at[c, j], s["ub_r"].at[c, j], partner)

    def gate_up(c):
        at, w = cuts[c]
        part = s["part%d" % c]
        for k, wt in enumerate(("wg", "wu")):
            r = jnp.dot(s["h"][...], s[wt][:, at:at + w], preferred_element_type=F32)
            part[:, :, :, k * w:(k + 1) * w] = r.reshape(nh, 2, 16, w)

        @pl.loop(0, nh)
        def _(j):
            s["s1_send%d" % c][j] = part[j, 1 - pa].astype(BF16)

        s1_copy(c).start()

    def pair_sum(c):
        s1_copy(c).wait_recv()
        part = s["part%d" % c]

        @pl.loop(1, nh)
        def _(i):
            j = lax.rem(ja + i, nh)
            s["s2_send%d" % c][j] = (part[j, pa] + s["s1_recv%d" % c][j].astype(F32)).astype(BF16)
            s2_copy(c, j).start()

    def make_units(c, inv):
        at, w = cuts[c]
        total = s["part%d" % c][ja, pa] + s["s1_recv%d" % c][ja].astype(F32)

        def body(i, total):
            j = lax.rem(ja + i, nh)
            blk = s["s2_recv%d" % c].at[j]
            remote(blk, blk, s["s2_s"].at[c, j], s["s2_r"].at[c, j], {"attn": 2 * j + pa, "ffn": f}).wait_recv()
            return total + blk[...].astype(F32)

        total = lax.fori_loop(1, nh, body, total)
        gate = total[:, :w] * inv
        up = total[:, w:] * inv
        s["u%d" % c][ja, pa] = (gate / (1.0 + jnp.exp(-gate)) * up).astype(BF16)

        @pl.loop(1, nh)
        def _(i):
            ua_copy(c, lax.rem(ja + i, nh)).start()

        ub_copy(c, ja).start()

    def forward(c):
        @pl.loop(1, nh)
        def _(i):
            j = lax.rem(ja + i, nh)
            blk = s["u%d" % c].at[j, pa]
            remote(blk, blk, s["ua_s"].at[c, j], s["ua_r"].at[c, j], {"attn": 2 * j + pa, "ffn": f}).wait_recv()
            ub_copy(c, j).start()

    def take_units(c):
        @pl.loop(0, nh)
        def _(j):
            blk = s["u%d" % c].at[j, 1 - pa]
            remote(blk, blk, s["ub_s"].at[c, j], s["ub_r"].at[c, j], partner).wait_recv()

    def down(c, t):
        at, w = cuts[c]
        mtd = min(512, tw)
        u = s["u%d" % c][...].reshape(rows, w)

        @pl.loop(0, tw // mtd)
        def _(k):
            col = pl.ds(pl.multiple_of(t * tw + k * mtd, mtd), mtd)
            loc = pl.ds(pl.multiple_of(k * mtd, mtd), mtd)
            r = jnp.dot(u, s["wd"][at:at + w, col], preferred_element_type=F32).reshape(n, 2, 8, mtd)
            if c > 0:
                r = r + s["down"][t, :, :, :, loc]
            s["down"][t, :, :, :, loc] = r

    cp_g.wait()
    cp_u.wait()
    gate_up(0)

    @pl.loop(1, n)
    def _(i):
        b = lax.rem(a + i, n)
        blk = s["sq_recv"].at[b]
        remote(blk, blk, s["sq_s"].at[b], s["sq_r"].at[b], {"attn": b, "ffn": f}).wait_recv()

    inv = lax.rsqrt(jnp.sum(s["sq_recv"][...], axis=0)[:1] / (n * cols) + EPS)
    s["inv"][...] = jnp.transpose(jnp.broadcast_to(inv, (128, rows)))

    @pl.loop(0, cols // mt)
    def _(t):
        c = pl.ds(pl.multiple_of(t * mt, mt), mt)
        mx = s["heads"][:, c] + s["hid"][:, c].astype(F32)
        s["h"][:, c] = (mx * s["inv"][:, :1] * gain_ref[c].astype(F32).reshape(1, mt)).astype(BF16)

    own_inv = s["inv"][pl.ds(pl.multiple_of(a * 16, 16), 16), :1]
    gate_up(1)
    pair_sum(0)
    gate_up(2)
    pair_sum(1)
    gate_up(3)
    make_units(0, own_inv)
    pair_sum(2)
    make_units(1, 1.0)
    forward(0)
    pair_sum(3)
    make_units(2, 1.0)
    forward(1)
    cp_d.wait()
    take_units(0)
    for t in range(TILES):
        down(0, t)
    make_units(3, 1.0)
    forward(2)
    take_units(1)
    for t in range(TILES):
        down(1, t)
    forward(3)
    take_units(2)
    for t in range(TILES):
        down(2, t)
    take_units(3)

    def sib_copy(t):
        return remote(s["down"].at[t, :, 1 - f], s["sib_recv"].at[t], s["sib_s"].at[t], s["sib_r"].at[t], sibling)

    def fin_copy(t, b):
        return remote(s["fin_send"].at[t, b], s["fin_recv"].at[t, a], s["fin_s"].at[t, b], s["fin_r"].at[t, a],
                      {"attn": b, "ffn": f})

    for t in range(TILES):
        down(3, t)
        sib_copy(t).start()
    for t in range(TILES):
        sib_copy(t).wait_recv()

        def added(b):
            hp = s["heads"][pl.ds(pl.multiple_of(b * 16, 16), 16), t * tw:(t + 1) * tw]
            hp = jnp.where(f == 0, hp[:8], hp[8:])
            return fold(s["down"][t, b, f] + s["sib_recv"][t, b] + hp)

        @pl.loop(1, n)
        def _(i):
            b = lax.rem(a + i, n)
            s["fin_send"][t, b] = added(b).astype(BF16)
            fin_copy(t, b).start()

        s["fin_recv"][t, a] = added(a).astype(BF16)

    def put(b):
        for t in range(TILES):
            y = unfold(s["hid_recv"][b, t].astype(F32) + s["fin_recv"][t, b].astype(F32))
            out_ref[:, pl.ds(pl.multiple_of(b * cols + t * tw, tw), tw)] = y

    put(a)

    @pl.loop(1, n)
    def _(i):
        b = lax.rem(a + i, n)
        blk = s["hid_recv"].at[b]
        remote(blk, blk, s["hid_s"].at[b], s["hid_r"].at[b], {"attn": b, "ffn": f}).wait_recv()
        for t in range(TILES):
            blk = s["fin_recv"].at[t, b]
            remote(blk, blk, s["fin_s"].at[t, b], s["fin_r"].at[t, b], {"attn": b, "ffn": f}).wait_recv()
        put(b)

    @pl.loop(1, nh)
    def _(i):
        aa_copy(lax.rem(ja + i, nh)).wait_send()

    @pl.loop(0, nh)
    def _(j):
        ab_copy(j).wait_send()
        for par in range(2):
            ac_copy(j, par).wait_send()

    @pl.loop(1, n)
    def _(i):
        b = lax.rem(a + i, n)
        hid_copy(b).wait_send()
        sq_copy(b).wait_send()
        for t in range(TILES):
            fin_copy(t, b).wait_send()

    for c in range(len(cuts)):
        s1_copy(c).wait_send()
        ub_copy(c, ja).wait_send()

        @pl.loop(1, nh)
        def _(i):
            j = lax.rem(ja + i, nh)
            s2_copy(c, j).wait_send()
            ua_copy(c, j).wait_send()
            ub_copy(c, j).wait_send()

    for t in range(TILES):
        sib_copy(t).wait_send()


def per_device(n, queries, kv_cache, lengths, hidden, out_weight, norm_gain, gate_weight, up_weight, down_weight):
    req, width = queries.shape
    slots, hd = kv_cache.shape[1:]
    rows, cols = hidden.shape
    units = gate_weight.shape[1]
    nh = n // 2
    tw = cols // TILES
    cuts = unit_chunks(units)
    nc = len(cuts)
    V, D = pltpu.VMEM, pltpu.SemaphoreType.DMA
    sc = {
        "k": V((slots, hd), BF16), "v": V((slots, hd), BF16), "hid": V((rows, cols), BF16),
        "wo": V(out_weight.shape, BF16), "wg": V(gate_weight.shape, BF16), "wu": V(up_weight.shape, BF16),
        "wd": V(down_weight.shape, BF16), "sc": V((req * width // hd, slots), F32),
        "hid_send": V((n, TILES, 16, tw // 2), BF16), "hid_recv": V((n, TILES, 16, tw // 2), BF16),
        "att": V((nh, 2, 2, 16, width // 2), BF16), "heads_in": V((rows, width), BF16),
        "heads": V((rows, cols), F32), "h": V((rows, cols), BF16),
        "sq_recv": V((n, 8, rows), F32), "inv": V((rows, 128), F32),
        "down": V((TILES, n, 2, 8, tw), F32), "sib_recv": V((TILES, n, 8, tw), F32),
        "fin_send": V((TILES, n, 16, tw // 2), BF16), "fin_recv": V((TILES, n, 16, tw // 2), BF16),
        "loc": D((7,)), "aa_s": D((nh,)), "aa_r": D((nh,)), "ab_s": D((nh,)), "ab_r": D((nh,)),
        "ac_s": D((nh, 2)), "ac_r": D((nh, 2)), "hid_s": D((n,)), "hid_r": D((n,)),
        "sq_s": D((n,)), "sq_r": D((n,)), "s1_s": D((nc,)), "s1_r": D((nc,)),
        "s2_s": D((nc, nh)), "s2_r": D((nc, nh)), "ua_s": D((nc, nh)), "ua_r": D((nc, nh)),
        "ub_s": D((nc, nh)), "ub_r": D((nc, nh)), "sib_s": D((TILES,)), "sib_r": D((TILES,)),
        "fin_s": D((TILES, n)), "fin_r": D((TILES, n)),
    }
    for c, (_, w) in enumerate(cuts):
        sc["part%d" % c] = V((nh, 2, 16, 2 * w), F32)
        for name in ("s1_send", "s1_recv", "s2_send", "s2_recv"):
            sc["%s%d" % (name, c)] = V((nh, 16, 2 * w), BF16)
        sc["u%d" % c] = V((nh, 2, 16, w), BF16)
    hbm = pl.BlockSpec(memory_space=pl.ANY)
    vmem = pl.BlockSpec(memory_space=pltpu.VMEM)
    smem = pl.BlockSpec(memory_space=pltpu.SMEM)
    return pl.pallas_call(
        functools.partial(kernel, n, tuple(sc)),
        out_shape=jax.ShapeDtypeStruct((req, cols * n), F32),
        in_specs=[vmem, hbm, smem, hbm, hbm, vmem, hbm, hbm, hbm],
        out_specs=vmem,
        scratch_shapes=list(sc.values()),
        compiler_params=pltpu.CompilerParams(collective_id=0, has_side_effects=True,
                                             vmem_limit_bytes=58 * 1024 * 1024),
    )(queries, kv_cache, lengths, hidden, out_weight, norm_gain, gate_weight, up_weight, down_weight)


def solution(mesh):
    return jax.shard_map(
        functools.partial(per_device, mesh.shape["attn"]),
        mesh=mesh,
        in_specs=(
            P(("groups", "attn", "ffn"), None),
            P(None, ("groups", "attn", "ffn"), None),
            P(("groups", "attn", "ffn")),
            P("groups", "attn"),
            P(None, "attn"),
            P("attn"),
            P("attn", "ffn"),
            P("attn", "ffn"),
            P("ffn", "attn"),
        ),
        out_specs=P(("groups", "attn", "ffn"), None),
        check_vma=False,
    )
```
